32 devices in a mesh: branch: 8 (over z, x), tensor: 4 (over y, core).
Axes of the slice: x: 2, y: 2, z: 4, core: 2. Of those that a mesh axis runs over, the one named last changes fastest.
Arguments:
- hidden: bfloat16 [1024, 4, 4096], P('branch', None, 'tensor'), may hold values from -6 to 6
- gain: float32 [4096], replicated, may hold values from 0.5 to 1.5
- w_query: bfloat16 [4096, 4096], P(None, 'tensor'), may hold values from -0.09375 to 0.09375
- w_keyval: bfloat16 [2, 4096, 1024], P(None, None, 'tensor'), may hold values from -0.09375 to 0.09375
- w_out: bfloat16 [4096, 4096], P('tensor'), may hold values from -0.09375 to 0.09375
- kv_codes: bfloat16 [256, 2, 64, 1024], P('branch', None, None, 'tensor'), may hold values from -12 to 12
- kv_scales: bfloat16 [256, 2, 8], P('branch', None, 'tensor'), may hold values from 0.5 to 24
- fork_export: int32 [64], P('branch'), may hold values from 0 to 31
- fork_pull: int32 [8, 64], replicated, may hold values from 0 to 63, as said below
- page_table: int32 [1024, 8], P('branch'), may hold values from 0 to 95
- lengths: int32 [1024], P('branch'), may hold values from 1 to 512, as said below
Outputs:
- mixed: bfloat16 [1024, 4, 4096], P('branch', None, 'tensor')
The draws below stay inside these ranges and needn't reach their ends.
Inputs may be any that keep to these rules, and one draw needn't show every extreme that they name: `fork_pull`: an entry s * 8 + e names offered page e of group s. In each row at most 16 entries name one group, and some group is named exactly 16 times in every row. `lengths`: some branch has exactly 512 tokens.
All inputs are finite; a program needn't handle non-finite values.
Results may differ from the reference program's by a relative error of at most 0.017.
Values may be sent and summed in bfloat16 or wider, within the bound.
A program may use at most 128 MiB of HBM per device.

```python
import math
import jax
import jax.numpy as jnp
from jax import lax

D = 4096
HEADS = 32
KVH = 8
HD = 128
PAGE = 64
STEPS = 4
BR_DEV = 128
MAXP = 8
OWN_PAGES = 32
FORK_DEV = 64
EXPORT = 8
CAP = 16
BRANCHES = 1024
POOL_PAGES = 256
EXPORTS = 64
N_BRANCH = 8
N_TENSOR = 4


def draw_kv_scales(key, part):
    key = jax.random.fold_in(key, 11)
    shape = (N_BRANCH * OWN_PAGES, 2, KVH)
    base = jnp.exp(jax.random.uniform(key, shape, jnp.float32, math.log(0.5), math.log(2.0)))
    return base.astype(jnp.bfloat16)


def draw_fork_pull(key, part):
    key = jax.random.fold_in(key, 17)
    row_keys = jax.random.split(key, N_BRANCH)

    def one_row(row_key):
        order = jax.random.permutation(row_key, N_BRANCH).astype(jnp.int32)
        source = order[jnp.arange(FORK_DEV) // CAP]
        entry = jax.random.randint(jax.random.fold_in(row_key, 1), (FORK_DEV,), 0, EXPORT)
        return (source * EXPORT + entry).astype(jnp.int32)
    return jax.vmap(one_row)(row_keys)


def draw_lengths(key, part):
    key = jax.random.fold_in(key, 23)
    most = MAXP * PAGE
    total = N_BRANCH * BR_DEV
    group_top = jax.random.randint(jax.random.fold_in(key, 1), (N_BRANCH,), most // 4 + 1, most + 1)
    tops = jnp.repeat(group_top, BR_DEV)
    values = jax.random.randint(key, (total,), 1, tops + 1)
    spot = jax.random.randint(jax.random.fold_in(key, 2), (), 0, total)
    return jnp.where(jnp.arange(total) == spot, most, values).astype(jnp.int32)


def plant(drawn, rng, low, top_value):
    shape = drawn.shape
    place = [jax.random.randint(jax.random.fold_in(rng, axis), (), 0, shape[axis]) for axis in range(len(shape))]
    drawn = drawn.at[tuple(place)].set(low)
    longest = shape.index(max(shape))
    place[longest] = (place[longest] + 1) % shape[longest]
    return drawn.at[tuple(place)].set(top_value)


def level_of(stream_key, dims, cuts, smallest, top_value):
    level = 1.0
    for position, parts in cuts:
        steps = jax.random.uniform(jax.random.fold_in(jax.random.fold_in(stream_key, 6), position), (parts,), jnp.float32, smallest / len(cuts), top_value / len(cuts))
        level = level * jnp.repeat(jnp.exp(steps), dims[position] // parts).reshape((-1,) + (1,) * (len(dims) - 1 - position))
    return level


def centred(stream_key, dims, deviation, bound, cuts=(), kind=jnp.bfloat16):
    loudness = level_of(stream_key, dims, cuts, -0.22, 0.18) if cuts else 1.0
    values = jax.random.normal(stream_key, dims, jnp.float32) * deviation * loudness
    return jnp.minimum(jnp.maximum(values, -bound), bound).astype(kind)


def setup_inputs(seed: int = 0) -> dict:
    key_list = jax.random.split(jax.random.key(seed), 12)
    hidden = centred(key_list[0], (BRANCHES, STEPS, D), 1.0, 6.0, ((0, 8), (2, 4)))
    gain = jnp.clip(1.0 + 0.1 * jax.random.normal(key_list[1], (D,), jnp.float32), 0.5, 1.5)
    w_query = centred(key_list[2], (D, HEADS * HD), D ** -0.5, 0.09375, ((1, 4),))
    w_keyval = centred(key_list[3], (2, D, KVH * HD), D ** -0.5, 0.09375, ((2, 4),))
    w_out = centred(key_list[4], (HEADS * HD, D), (HEADS * HD) ** -0.5, 0.09375, ((0, 4),))
    kv_codes = centred(key_list[5], (POOL_PAGES, 2, PAGE, KVH * HD), 2.0, 12.0, ((0, 8), (3, 4)))
    kv_scales = draw_kv_scales(jax.random.fold_in(key_list[11], 71), 0)
    fork_export = plant(jax.random.randint(key_list[7], (EXPORTS,), 0, OWN_PAGES), jax.random.fold_in(key_list[7], 1), 0, OWN_PAGES - 1).astype(jnp.int32)
    fork_pull = draw_fork_pull(jax.random.fold_in(key_list[11], 71), 0)
    page_table = plant(jax.random.randint(key_list[9], (BRANCHES, MAXP), 0, FORK_DEV + OWN_PAGES), jax.random.fold_in(key_list[9], 1), 0, (FORK_DEV + OWN_PAGES) - 1).astype(jnp.int32)
    lengths = draw_lengths(jax.random.fold_in(key_list[11], 71), 0)
    return dict(hidden=hidden, gain=gain, w_query=w_query, w_keyval=w_keyval, w_out=w_out, kv_codes=kv_codes, kv_scales=kv_scales, fork_export=fork_export, fork_pull=fork_pull, page_table=page_table, lengths=lengths)


def rotate(values, positions):
    half = values.shape[-1] // 2
    freq = jnp.exp(-(2.0 * jnp.arange(half).astype(jnp.float32) / values.shape[-1]) * math.log(500000.0))
    angle = positions.astype(jnp.float32)[:, None] * freq[None, :]
    cosine = jnp.cos(angle)[:, None, :]
    sine = jnp.sin(angle)[:, None, :]
    first = values[..., :half]
    second = values[..., half:]
    return jnp.concatenate([first * cosine - second * sine, second * cosine + first * sine], axis=-1)

def attend_block(query, key_new, value_new, codes, scales, lengths_block):
    blocks, slots, page = (codes.shape[0], codes.shape[1], codes.shape[3])
    heads_here = query.shape[2]
    steps = query.shape[1]
    keys = codes[:, :, 0].reshape(blocks, slots, page, heads_here, HD).astype(jnp.float32)
    values = codes[:, :, 1].reshape(blocks, slots, page, heads_here, HD).astype(jnp.float32)
    key_scale = jnp.transpose(scales[:, :, 0].astype(jnp.float32), (0, 2, 1))[:, None, :, None, :, None]
    value_scale = jnp.transpose(scales[:, :, 1].astype(jnp.float32), (0, 2, 1))[:, None, :, None, :, None]
    query_f = query.astype(jnp.float32)
    context = jnp.einsum('bthgd,bmphd->bthgmp', query_f, keys) * key_scale
    token = jnp.arange(slots).astype(jnp.int32)[:, None] * page + jnp.arange(page).astype(jnp.int32)[None, :]
    live = (token[None, :, :] < lengths_block[:, None, None])[:, None, None, None, :, :]
    fresh = jnp.einsum('bthgd,bshd->bthgs', query_f, key_new.astype(jnp.float32))
    causal = (jnp.arange(steps)[:, None] >= jnp.arange(steps)[None, :])[None, :, None, None, :]
    context = jnp.where(live, context, -1e+30)
    fresh = jnp.where(causal, fresh, -1e+30)
    top = jnp.maximum(lax.optimization_barrier(jnp.max(context, axis=(4, 5))), lax.optimization_barrier(jnp.max(fresh, axis=4)))
    context_exp = jnp.where(live, jnp.exp(context - top[..., None, None]), 0.0)
    fresh_exp = jnp.where(causal, jnp.exp(fresh - top[..., None]), 0.0)
    total = lax.optimization_barrier(jnp.sum(context_exp, axis=(4, 5))) + lax.optimization_barrier(jnp.sum(fresh_exp, axis=4))
    context_w = (context_exp / total[..., None, None] * value_scale).astype(jnp.bfloat16)
    fresh_w = (fresh_exp / total[..., None]).astype(jnp.bfloat16)
    result = jnp.einsum('bthgmp,bmphd->bthgd', context_w.astype(jnp.float32), values)
    result = result + jnp.einsum('bthgs,bshd->bthgd', fresh_w.astype(jnp.float32), value_new.astype(jnp.float32))
    return result.astype(jnp.bfloat16)

def reference(hidden, gain, w_query, w_keyval, w_out, kv_codes, kv_scales, fork_export, fork_pull, page_table, lengths):
    branches = hidden.shape[0]
    group = HEADS // KVH
    rows = hidden.astype(jnp.float32).reshape(branches * STEPS, D)
    power = lax.optimization_barrier(jnp.mean(rows * rows, axis=-1, keepdims=True))
    normed = (rows * lax.rsqrt(power + 1e-05) * gain).astype(jnp.bfloat16)
    positions = (lengths[:, None] + jnp.arange(STEPS).astype(jnp.int32)[None, :]).reshape(-1)
    query = jnp.dot(normed, w_query, preferred_element_type=jnp.float32).reshape(-1, HEADS, HD)
    query = (rotate(query, positions) * HD ** (-0.5)).astype(jnp.bfloat16).reshape(branches, STEPS, KVH, group, HD)
    key_new = jnp.dot(normed, w_keyval[0], preferred_element_type=jnp.float32).reshape(-1, KVH, HD)
    key_new = rotate(key_new, positions).astype(jnp.bfloat16).reshape(branches, STEPS, KVH, HD)
    value_new = jnp.dot(normed, w_keyval[1], preferred_element_type=jnp.float32).astype(jnp.bfloat16).reshape(branches, STEPS, KVH, HD)
    parents = fork_pull // EXPORT * OWN_PAGES + fork_export[fork_pull]
    owned = jnp.arange(N_BRANCH).astype(jnp.int32)[:, None] * OWN_PAGES + jnp.arange(OWN_PAGES).astype(jnp.int32)[None, :]
    pool = jnp.concatenate([parents.astype(jnp.int32), owned], axis=1)
    owner = jnp.arange(branches).astype(jnp.int32) // BR_DEV
    context = pool[owner[:, None], page_table]
    block = 8
    count = branches // block

    def shaped(array):
        return array.reshape((count, block) + array.shape[1:])

    def one_block(items):
        pages, lens, query_b, key_b, value_b = items
        return attend_block(query_b, key_b, value_b, kv_codes[pages], kv_scales[pages], lens)
    attended = lax.map(one_block, (shaped(context), shaped(lengths), shaped(query), shaped(key_new), shaped(value_new)))
    attended = attended.reshape(branches * STEPS, HEADS * HD)
    inner = HEADS * HD // N_TENSOR
    total = jnp.zeros((branches * STEPS, D), jnp.float32)
    for index in range(N_TENSOR):
        partial_sum = jnp.dot(attended[:, index * inner:(index + 1) * inner], w_out[index * inner:(index + 1) * inner], preferred_element_type=jnp.float32).astype(jnp.bfloat16)
        partial_sum = lax.optimization_barrier(partial_sum)
        total = total + partial_sum.astype(jnp.float32)
    return total.astype(jnp.bfloat16).reshape(branches, STEPS, D)
```

```python
import functools
import math

import jax
import jax.numpy as jnp
from jax import lax
from jax.experimental import pallas as pl
from jax.experimental.pallas import tpu as pltpu
from jax.sharding import PartitionSpec as P

HEADS = 32
KVH = 8
HD = 128
STEPS = 4
GROUP = HEADS // KVH
NT = (((1,), (1,)), ((), ()))


def project_kernel(hid_ref, gain_ref, cos_ref, sin_ref, wq_ref, wkv_ref, q_ref, kn_ref, vn_ref,
                   weights, kv_weights, normed, tmp, q_rows, sems):
    parts, rows, width = hid_ref.shape
    branches = rows // STEPS
    q_tiles = wq_ref.shape[1] // 256
    copies = []
    for c in range(q_tiles):
        copies.append(pltpu.make_async_copy(wq_ref.at[:, pl.ds(c * 256, 256)], weights.at[c], sems.at[c]))
    for c in range(2):
        copies.append(pltpu.make_async_copy(wkv_ref.at[c], kv_weights.at[c], sems.at[q_tiles + c]))
    for copy in copies:
        copy.start()

    def norm_rows(r, _):
        at = pl.ds(pl.multiple_of(r * 64, 64), 64)
        power = jnp.zeros((64, 1), jnp.float32)
        for k in range(parts):
            v = hid_ref[k, at, :].astype(jnp.float32)
            power += jnp.sum(v * v, axis=-1, keepdims=True)
        inv = lax.rsqrt(power / (parts * width) + 1e-05)
        for k in range(parts):
            v = hid_ref[k, at, :].astype(jnp.float32)
            normed[at, k * width : (k + 1) * width] = (v * inv * gain_ref[k : k + 1, :]).astype(jnp.bfloat16)
        return 0

    lax.fori_loop(0, rows // 64, norm_rows, 0)

    def rope(v):
        return v * cos_ref[...] + pltpu.roll(v, HD // 2, 1) * sin_ref[...]

    for c in range(q_tiles + 2):
        copies[c].wait()
        tile = weights[c] if c < q_tiles else kv_weights[c - q_tiles]
        acc = jnp.dot(normed[...], tile, preferred_element_type=jnp.float32)
        if c < q_tiles:
            for i in range(2):
                tmp[...] = rope(acc[:, i * HD : (i + 1) * HD]) * HD ** (-0.5)
                head = c * 2 + i
                for t in range(STEPS):
                    q_rows[pl.ds(head * STEPS + t, branches, stride=q_tiles * 2 * STEPS), :] = tmp[
                        pl.ds(t, branches, stride=STEPS), :
                    ]
        elif c == q_tiles:
            for i in range(kv_weights.shape[2] // HD):
                kn_ref[:, i * HD : (i + 1) * HD] = rope(acc[:, i * HD : (i + 1) * HD]).astype(jnp.bfloat16)
        else:
            vn_ref[...] = acc.astype(jnp.bfloat16)
    q_ref[...] = q_rows[...].astype(jnp.bfloat16)


def attend_kernel(table_ref, lens_ref, q_ref, kn_ref, vn_ref, scale_ref, far_ref, own_ref, wo_ref,
                  out_ref, pool, scales, att_rows, tmp, att, sems):
    groups, far_rows = far_ref.shape[:2]
    own = own_ref.shape[0]
    per = (pool.shape[0] - own) // groups
    page = pool.shape[2]
    branches = lens_ref.shape[0]
    slots = table_ref.shape[0] // branches
    span = slots * page
    copies = [pltpu.make_async_copy(own_ref, pool.at[pl.ds(groups * per, own)], sems.at[groups])]
    for g in range(groups):
        copies.append(pltpu.make_async_copy(far_ref.at[g], pool.at[pl.ds(g * per, per)], sems.at[g]))
    for copy in copies:
        copy.start()
    spread = (
        lax.broadcasted_iota(jnp.int32, (slots, span), 1) // page
        == lax.broadcasted_iota(jnp.int32, (slots, span), 0)
    ).astype(jnp.bfloat16)
    scales[...] = jnp.dot(scale_ref[...], spread, preferred_element_type=jnp.float32)
    for copy in copies:
        copy.wait()

    kv_heads = kn_ref.shape[1] // HD
    deep = GROUP * STEPS
    each = deep * kv_heads
    row = lax.broadcasted_iota(jnp.int32, (8 * each, 1), 0)
    kv_head = (row % each) // deep
    col = lax.broadcasted_iota(jnp.int32, (8 * each, 32), 1)
    seen = ((col // STEPS) == (row // each)) & ((col % STEPS) <= (row % STEPS))
    token = lax.broadcasted_iota(jnp.int32, (1, span), 1)

    def block(b, _):
        at = pl.ds(pl.multiple_of(b * 8 * each, 8 * each), 8 * each)
        q = q_ref[at, :]
        zero = jnp.zeros_like(q)
        wide = jnp.concatenate([jnp.where(kv_head == h, q, zero) for h in range(kv_heads)], axis=1)
        new = pl.ds(pl.multiple_of(b * 32, 32), 32)
        fresh = lax.dot_general(wide, kn_ref[new, :], NT, preferred_element_type=jnp.float32)
        fresh = jnp.where(seen, fresh, -1e30)
        fresh_top = jnp.max(fresh, axis=1, keepdims=True)
        outs, tops, sums = [], [], []
        for i in range(8):
            n = b * 8 + i
            ids = [table_ref[n * slots + m] for m in range(slots)]
            keys = jnp.concatenate([pool[x, 0] for x in ids], axis=0)
            s = lax.dot_general(wide[i * each : (i + 1) * each], keys, NT, preferred_element_type=jnp.float32)
            sc = scales[pl.ds(pl.multiple_of(n * 8, 8), 8), :]
            ks, vs = (
                jnp.concatenate(
                    [
                        jnp.broadcast_to(sc[j * kv_heads + h : j * kv_heads + h + 1], (deep, span))
                        for h in range(kv_heads)
                    ],
                    axis=0,
                )
                for j in range(2)
            )
            s = jnp.where(token < lens_ref[n], s * ks, -1e30)
            top = jnp.maximum(jnp.max(s, axis=1, keepdims=True), fresh_top[i * each : (i + 1) * each])
            e = jnp.exp(s - top)
            tops.append(top)
            sums.append(jnp.sum(e, axis=1, keepdims=True))
            values = jnp.concatenate([pool[x, 1] for x in ids], axis=0)
            outs.append(
                jnp.dot((e * vs).astype(jnp.bfloat16), values, preferred_element_type=jnp.float32)
            )
        fresh_e = jnp.exp(fresh - jnp.concatenate(tops, axis=0))
        total = jnp.concatenate(sums, axis=0) + jnp.sum(fresh_e, axis=1, keepdims=True)
        out = jnp.concatenate(outs, axis=0) + jnp.dot(
            fresh_e.astype(jnp.bfloat16), vn_ref[new, :], preferred_element_type=jnp.float32
        )
        picked = out[:, :HD]
        for h in range(1, kv_heads):
            picked = jnp.where(kv_head == h, out[:, h * HD : (h + 1) * HD], picked)
        att_rows[at, :] = picked / total
        return 0

    lax.fori_loop(0, branches // 8, block, 0)

    heads = att.shape[1] // HD
    for head in range(heads):
        for t in range(STEPS):
            tmp[pl.ds(t, branches, stride=STEPS), :] = att_rows[
                pl.ds(head * STEPS + t, branches, stride=heads * STEPS), :
            ]
        att[:, head * HD : (head + 1) * HD] = tmp[...].astype(jnp.bfloat16)

    parts = out_ref.shape[0]
    width = out_ref.shape[2]

    def project(j, _):
        for k in range(parts):
            cols = pl.ds(pl.multiple_of(k * width + j * 256, 256), 256)
            out_ref[k, :, pl.ds(pl.multiple_of(j * 256, 256), 256)] = jnp.dot(
                att[...], wo_ref[:, cols], preferred_element_type=jnp.float32
            ).astype(jnp.bfloat16)
        return 0

    lax.fori_loop(0, width // 256, project, 0)


def per_device(hidden, gain, w_query, w_keyval, w_out, kv_codes, kv_scales, fork_export, fork_pull,
               page_table, lengths):
    branches, steps, width = hidden.shape
    rows = branches * steps
    parts = lax.axis_size("tensor")
    own, _, page, kv_cols = kv_codes.shape
    per = fork_export.shape[0]
    heads_here = kv_cols // HD
    full = lax.all_gather(hidden.reshape(rows, width), "tensor", axis=0, tiled=False)

    positions = (lengths[:, None] + jnp.arange(steps, dtype=jnp.int32)[None, :]).reshape(-1)
    half = HD // 2
    freq = jnp.exp(-(2.0 * jnp.arange(half).astype(jnp.float32) / HD) * math.log(500000.0))
    angle = positions.astype(jnp.float32)[:, None] * freq[None, :]
    cosine, sine = jnp.cos(angle), jnp.sin(angle)
    cosine = jnp.concatenate([cosine, cosine], axis=1)
    sine = jnp.concatenate([-sine, sine], axis=1)

    myself = lax.axis_index("branch")
    my_row = lax.dynamic_index_in_dim(fork_pull, myself, 0, keepdims=False)
    offered = kv_codes[fork_export].reshape(per * 2 * page, kv_cols)
    tail = jnp.zeros((16, kv_cols), jnp.bfloat16)
    tail = tail.at[0, : per * 2 * heads_here].set(kv_scales[fork_export].reshape(-1))
    every = lax.all_gather(jnp.concatenate([offered, tail], axis=0), "branch", axis=0, tiled=False)
    groups = every.shape[0]
    far = every[:, : per * 2 * page].reshape(groups, per, 2, page, kv_cols)
    far_scales = every[:, per * 2 * page, : per * 2 * heads_here].reshape(groups * per, 2 * heads_here)

    pool_ids = jnp.concatenate([my_row, jnp.arange(own, dtype=jnp.int32) + groups * per])
    pool_scales = jnp.concatenate([far_scales, kv_scales.reshape(own, 2 * heads_here)], axis=0)
    table = pool_ids[page_table]
    slots = table.shape[1]
    scale = jnp.pad(jnp.transpose(pool_scales[table], (0, 2, 1)), ((0, 0), (0, 8 - 2 * heads_here), (0, 0)))
    scale = scale.reshape(branches * 8, slots)

    heads = w_query.shape[1] // HD
    q_tiles = w_query.shape[1] // 256
    vmem = pl.BlockSpec(memory_space=pltpu.VMEM)
    anywhere = pl.BlockSpec(memory_space=pl.ANY)
    smem = pl.BlockSpec(memory_space=pltpu.SMEM)
    query, key_new, value_new = pl.pallas_call(
        project_kernel,
        out_shape=(
            jax.ShapeDtypeStruct((branches * heads * steps, HD), jnp.bfloat16),
            jax.ShapeDtypeStruct((rows, kv_cols), jnp.bfloat16),
            jax.ShapeDtypeStruct((rows, kv_cols), jnp.bfloat16),
        ),
        in_specs=[vmem, vmem, vmem, vmem, anywhere, anywhere],
        out_specs=(vmem, vmem, vmem),
        scratch_shapes=[
            pltpu.VMEM((q_tiles, parts * width, 256), jnp.bfloat16),
            pltpu.VMEM((2, parts * width, kv_cols), jnp.bfloat16),
            pltpu.VMEM((rows, parts * width), jnp.bfloat16),
            pltpu.VMEM((rows, HD), jnp.float32),
            pltpu.VMEM((branches * heads * steps, HD), jnp.float32),
            pltpu.SemaphoreType.DMA((q_tiles + 2,)),
        ],
        compiler_params=pltpu.CompilerParams(vmem_limit_bytes=48 * 2**20),
    )(full, gain.reshape(parts, width), cosine, sine, w_query, w_keyval)

    partial = pl.pallas_call(
        attend_kernel,
        out_shape=jax.ShapeDtypeStruct((parts, rows, width), jnp.bfloat16),
        in_specs=[smem, smem, vmem, vmem, vmem, vmem, anywhere, anywhere, vmem],
        out_specs=vmem,
        scratch_shapes=[
            pltpu.VMEM((groups * per + own, 2, page, kv_cols), jnp.bfloat16),
            pltpu.VMEM((branches * 8, slots * page), jnp.float32),
            pltpu.VMEM((branches * heads * steps, HD), jnp.float32),
            pltpu.VMEM((rows, HD), jnp.float32),
            pltpu.VMEM((rows, heads * HD), jnp.bfloat16),
            pltpu.SemaphoreType.DMA((groups + 1,)),
        ],
        compiler_params=pltpu.CompilerParams(vmem_limit_bytes=48 * 2**20),
    )(table.reshape(-1), lengths, query, key_new, value_new, scale, far, kv_codes, w_out)
    mixed = lax.psum_scatter(partial, "tensor", scatter_dimension=0, tiled=False)
    return mixed.reshape(branches, steps, width)


def solution(mesh):
    return jax.shard_map(
        per_device,
        mesh=mesh,
        in_specs=(
            P("branch", None, "tensor"),
            P(),
            P(None, "tensor"),
            P(None, None, "tensor"),
            P("tensor", None),
            P("branch", None, None, "tensor"),
            P("branch", None, "tensor"),
            P("branch"),
            P(),
            P("branch", None),
            P("branch"),
        ),
        out_specs=P("branch", None, "tensor"),
        check_vma=False,
    )
```

```python
import functools
import math

import jax
import jax.numpy as jnp
from jax import lax
from jax.experimental import pallas as pl
from jax.experimental.pallas import tpu as pltpu
from jax.sharding import PartitionSpec as P

HEADS = 32
KVH = 8
HD = 128
STEPS = 4
GROUP = HEADS // KVH
NT = (((1,), (1,)), ((), ()))


def project_kernel(hid_ref, gain_ref, cos_ref, sin_ref, wq_ref, wkv_ref, q_ref, kn_ref, vn_ref,
                   weights, kv_weights, normed, tmp, q_rows, sems):
    parts, rows, width = hid_ref.shape
    branches = rows // STEPS
    q_tiles = wq_ref.shape[1] // 256
    copies = []
    for c in range(q_tiles):
        copies.append(pltpu.make_async_copy(wq_ref.at[:, pl.ds(c * 256, 256)], weights.at[c], sems.at[c]))
    for c in range(2):
        copies.append(pltpu.make_async_copy(wkv_ref.at[c], kv_weights.at[c], sems.at[q_tiles + c]))
    for copy in copies:
        copy.start()

    def norm_rows(r, _):
        at = pl.ds(pl.multiple_of(r * 64, 64), 64)
        power = jnp.zeros((64, 1), jnp.float32)
        for k in range(parts):
            v = hid_ref[k, at, :].astype(jnp.float32)
            power += jnp.sum(v * v, axis=-1, keepdims=True)
        inv = lax.rsqrt(power / (parts * width) + 1e-05)
        for k in range(parts):
            v = hid_ref[k, at, :].astype(jnp.float32)
            normed[at, k * width : (k + 1) * width] = (v * inv * gain_ref[k : k + 1, :]).astype(jnp.bfloat16)
        return 0

    lax.fori_loop(0, rows // 64, norm_rows, 0)

    def rope(v):
        return v * cos_ref[...] + pltpu.roll(v, HD // 2, 1) * sin_ref[...]

    for c in range(q_tiles + 2):
        copies[c].wait()
        tile = weights[c] if c < q_tiles else kv_weights[c - q_tiles]
        acc = jnp.dot(normed[...], tile, preferred_element_type=jnp.float32)
        if c < q_tiles:
            for i in range(2):
                tmp[...] = rope(acc[:, i * HD : (i + 1) * HD]) * HD ** (-0.5)
                head = c * 2 + i
                for t in range(STEPS):
                    q_rows[pl.ds(head * STEPS + t, branches, stride=q_tiles * 2 * STEPS), :] = tmp[
                        pl.ds(t, branches, stride=STEPS), :
                    ]
        elif c == q_tiles:
            for i in range(kv_weights.shape[2] // HD):
                kn_ref[:, i * HD : (i + 1) * HD] = rope(acc[:, i * HD : (i + 1) * HD]).astype(jnp.bfloat16)
        else:
            vn_ref[...] = acc.astype(jnp.bfloat16)
    q_ref[...] = q_rows[...].astype(jnp.bfloat16)


def offer_kernel(export_ref, codes_ref, tail_ref, out_ref, sems):
    per = export_ref.shape[0]
    rows = (out_ref.shape[0] - tail_ref.shape[0]) // per
    copies = [
        pltpu.make_async_copy(
            codes_ref.at[pl.ds(pl.multiple_of(export_ref[j] * rows, rows), rows)],
            out_ref.at[pl.ds(j * rows, rows)],
            sems.at[j],
        )
        for j in range(per)
    ]
    copies.append(
        pltpu.make_async_copy(tail_ref, out_ref.at[pl.ds(per * rows, tail_ref.shape[0])], sems.at[per])
    )
    for copy in copies:
        copy.start()
    for copy in copies:
        copy.wait()


def exchange_kernel(far, near, mine_ref, every_ref, local_sem, send_far, recv_far, send_near, recv_near):
    me = lax.axis_index("branch")
    line, place = me // near, me % near

    def far_peer(k):
        return ((line + k) % far) * near + place

    def near_peer(j):
        return line * near + (place + j) % near

    def push(src, block, peer, send_sem, recv_sem):
        copy = pltpu.make_async_remote_copy(
            src_ref=src,
            dst_ref=every_ref.at[block],
            send_sem=send_sem,
            recv_sem=recv_sem,
            device_id={"branch": peer},
            device_id_type=pl.DeviceIdType.MESH,
        )
        copy.start()
        return copy

    barrier = pltpu.get_barrier_semaphore()
    peers = [far_peer(k) for k in range(1, far)] + [near_peer(j) for j in range(1, near)]
    for peer in peers:
        pl.semaphore_signal(
            barrier, inc=1, device_id={"branch": peer}, device_id_type=pl.DeviceIdType.MESH
        )
    pl.semaphore_wait(barrier, len(peers))

    order = sorted(range(1, far), key=lambda k: min(k, far - k))
    sent_far = {k: push(mine_ref, me, far_peer(k), send_far.at[k - 1], recv_far.at[k - 1]) for k in order}
    sent_near = [
        push(mine_ref, me, near_peer(j), send_near.at[0, j - 1], recv_near.at[0, j - 1])
        for j in range(1, near)
    ]
    own = pltpu.make_async_copy(mine_ref, every_ref.at[me], local_sem)
    own.start()
    for k in order:
        sent_far[k].wait_recv()
        block = ((line + far - k) % far) * near + place
        for j in range(1, near):
            sent_near.append(
                push(
                    every_ref.at[block], block, near_peer(j), send_near.at[k, j - 1], recv_near.at[k, j - 1]
                )
            )
    for copy in sent_near:
        copy.wait_recv()
    for k in order:
        sent_far[k].wait_send()
    for copy in sent_near:
        copy.wait_send()
    own.wait()


def attend_kernel(begin, branches, table_ref, lens_ref, q_ref, kn_ref, vn_ref, scale_ref, far_ref, own_ref, wo_ref,
                  out_ref, pool, scales, att_rows, tmp, att, sems):
    groups = far_ref.shape[0]
    slots = table_ref.shape[0] // lens_ref.shape[0]
    page = scales.shape[1] // slots
    per = (pool.shape[0] - own_ref.shape[0]) // (groups * 2 * page)
    span = slots * page
    copies = [
        pltpu.make_async_copy(own_ref, pool.at[pl.ds(groups * per * 2 * page, own_ref.shape[0])], sems.at[groups])
    ]
    for g in range(groups):
        copies.append(pltpu.make_async_copy(far_ref.at[g, pl.ds(0, per * 2 * page)], pool.at[pl.ds(g * per * 2 * page, per * 2 * page)], sems.at[g]))
    for copy in copies:
        copy.start()
    spread = (
        lax.broadcasted_iota(jnp.int32, (slots, span), 1) // page
        == lax.broadcasted_iota(jnp.int32, (slots, span), 0)
    ).astype(jnp.bfloat16)
    scales[...] = jnp.dot(scale_ref[pl.ds(begin * 8, branches * 8), :], spread, preferred_element_type=jnp.float32)
    for copy in copies:
        copy.wait()

    kv_heads = kn_ref.shape[1] // HD
    deep = GROUP * STEPS
    each = deep * kv_heads
    row = lax.broadcasted_iota(jnp.int32, (8 * each, 1), 0)
    kv_head = (row % each) // deep
    col = lax.broadcasted_iota(jnp.int32, (8 * each, 32), 1)
    seen = ((col // STEPS) == (row // each)) & ((col % STEPS) <= (row % STEPS))
    token = lax.broadcasted_iota(jnp.int32, (1, span), 1)

    def block(b, _):
        at = pl.ds(pl.multiple_of(b * 8 * each, 8 * each), 8 * each)
        q = q_ref[pl.ds(pl.multiple_of(begin * each + b * 8 * each, 8 * each), 8 * each), :]
        zero = jnp.zeros_like(q)
        wide = jnp.concatenate([jnp.where(kv_head == h, q, zero) for h in range(kv_heads)], axis=1)
        new = pl.ds(pl.multiple_of(begin * STEPS + b * 32, 32), 32)
        fresh = lax.dot_general(wide, kn_ref[new, :], NT, preferred_element_type=jnp.float32)
        fresh = jnp.where(seen, fresh, -1e30)
        fresh_top = jnp.max(fresh, axis=1, keepdims=True)
        outs, tops, sums = [], [], []
        for i in range(8):
            n = begin + b * 8 + i
            ids = [table_ref[n * slots + m] for m in range(slots)]
            keys = jnp.concatenate([pool[pl.ds(pl.multiple_of(x * 2 * page, 2 * page), page), :] for x in ids], axis=0)
            s = lax.dot_general(wide[i * each : (i + 1) * each], keys, NT, preferred_element_type=jnp.float32)
            sc = scales[pl.ds(pl.multiple_of((n - begin) * 8, 8), 8), :]
            ks, vs = (
                jnp.concatenate(
                    [
                        jnp.broadcast_to(sc[j * kv_heads + h : j * kv_heads + h + 1], (deep, span))
                        for h in range(kv_heads)
                    ],
                    axis=0,
                )
                for j in range(2)
            )
            s = jnp.where(token < lens_ref[n], s * ks, -1e30)
            top = jnp.maximum(jnp.max(s, axis=1, keepdims=True), fresh_top[i * each : (i + 1) * each])
            e = jnp.exp(s - top)
            tops.append(top)
            sums.append(jnp.sum(e, axis=1, keepdims=True))
            values = jnp.concatenate([pool[pl.ds(pl.multiple_of(x * 2 * page + page, page), page), :] for x in ids], axis=0)
            outs.append(
                jnp.dot((e * vs).astype(jnp.bfloat16), values, preferred_element_type=jnp.float32)
            )
        fresh_e = jnp.exp(fresh - jnp.concatenate(tops, axis=0))
        total = jnp.concatenate(sums, axis=0) + jnp.sum(fresh_e, axis=1, keepdims=True)
        out = jnp.concatenate(outs, axis=0) + jnp.dot(
            fresh_e.astype(jnp.bfloat16), vn_ref[new, :], preferred_element_type=jnp.float32
        )
        picked = out[:, :HD]
        for h in range(1, kv_heads):
            picked = jnp.where(kv_head == h, out[:, h * HD : (h + 1) * HD], picked)
        att_rows[at, :] = picked / total
        return 0

    lax.fori_loop(0, branches // 8, block, 0)

    heads = att.shape[1] // HD
    for head in range(heads):
        for t in range(STEPS):
            tmp[pl.ds(t, branches, stride=STEPS), :] = att_rows[
                pl.ds(head * STEPS + t, branches, stride=heads * STEPS), :
            ]
        att[:, head * HD : (head + 1) * HD] = tmp[...].astype(jnp.bfloat16)

    parts = out_ref.shape[0]
    width = out_ref.shape[2]

    def project(j, _):
        for k in range(parts):
            cols = pl.ds(pl.multiple_of(k * width + j * 256, 256), 256)
            out_ref[k, :, pl.ds(pl.multiple_of(j * 256, 256), 256)] = jnp.dot(
                att[...], wo_ref[:, cols], preferred_element_type=jnp.float32
            ).astype(jnp.bfloat16)
        return 0

    lax.fori_loop(0, width // 256, project, 0)


def per_device(hidden, gain, w_query, w_keyval, w_out, kv_codes, kv_scales, fork_export, fork_pull,
               page_table, lengths):
    branches, steps, width = hidden.shape
    rows = branches * steps
    parts = lax.axis_size("tensor")
    own, _, page, kv_cols = kv_codes.shape
    per = fork_export.shape[0]
    heads_here = kv_cols // HD
    full = lax.all_gather(hidden.reshape(rows, width), "tensor", axis=0, tiled=False)

    positions = (lengths[:, None] + jnp.arange(steps, dtype=jnp.int32)[None, :]).reshape(-1)
    half = HD // 2
    freq = jnp.exp(-(2.0 * jnp.arange(half).astype(jnp.float32) / HD) * math.log(500000.0))
    angle = positions.astype(jnp.float32)[:, None] * freq[None, :]
    cosine, sine = jnp.cos(angle), jnp.sin(angle)
    cosine = jnp.concatenate([cosine, cosine], axis=1)
    sine = jnp.concatenate([-sine, sine], axis=1)

    myself = lax.axis_index("branch")
    my_row = lax.dynamic_index_in_dim(fork_pull, myself, 0, keepdims=False)
    vmem = pl.BlockSpec(memory_space=pltpu.VMEM)
    anywhere = pl.BlockSpec(memory_space=pl.ANY)
    smem = pl.BlockSpec(memory_space=pltpu.SMEM)
    groups = lax.axis_size("branch")
    near = 2 ** (int(math.log2(groups)) // 2)
    pages = kv_codes.reshape(own, 2 * page, kv_cols)
    tail = jnp.pad(
        kv_scales[fork_export].reshape(1, -1), ((0, 15), (0, kv_cols - per * 2 * heads_here))
    )
    offered = pl.pallas_call(
        offer_kernel,
        out_shape=jax.ShapeDtypeStruct((per * 2 * page + 16, kv_cols), jnp.bfloat16),
        in_specs=[smem, anywhere, anywhere],
        out_specs=anywhere,
        scratch_shapes=[pltpu.SemaphoreType.DMA((per + 1,))],
    )(fork_export, pages.reshape(own * 2 * page, kv_cols), tail)
    far_count = groups // near
    every = pl.pallas_call(
        functools.partial(exchange_kernel, far_count, near),
        out_shape=jax.ShapeDtypeStruct((groups,) + offered.shape, jnp.bfloat16),
        in_specs=[anywhere],
        out_specs=anywhere,
        scratch_shapes=[
            pltpu.SemaphoreType.DMA,
            pltpu.SemaphoreType.DMA((far_count - 1,)),
            pltpu.SemaphoreType.DMA((far_count - 1,)),
            pltpu.SemaphoreType.DMA((far_count, near - 1)),
            pltpu.SemaphoreType.DMA((far_count, near - 1)),
        ],
        compiler_params=pltpu.CompilerParams(collective_id=0, has_side_effects=True),
        cost_estimate=pl.CostEstimate(flops=0, bytes_accessed=150 * 2**20, transcendentals=0),
    )(offered)
    far_scales = every[:, per * 2 * page, : per * 2 * heads_here].reshape(groups * per, 2 * heads_here)

    pool_ids = jnp.concatenate([my_row, jnp.arange(own, dtype=jnp.int32) + groups * per])
    pool_scales = jnp.concatenate([far_scales, kv_scales.reshape(own, 2 * heads_here)], axis=0)
    table = pool_ids[page_table]
    slots = table.shape[1]
    chosen = (table[:, :, None] == jnp.arange(groups * per + own)).astype(jnp.bfloat16)
    padded = jnp.pad(pool_scales, ((0, 0), (0, 8 - 2 * heads_here)))
    scale = jnp.einsum("nmp,pj->njm", chosen, padded, preferred_element_type=jnp.float32).astype(jnp.bfloat16)
    scale = scale.reshape(branches * 8, slots)

    heads = w_query.shape[1] // HD
    q_tiles = w_query.shape[1] // 256
    query, key_new, value_new = pl.pallas_call(
        project_kernel,
        out_shape=(
            jax.ShapeDtypeStruct((branches * heads * steps, HD), jnp.bfloat16),
            jax.ShapeDtypeStruct((rows, kv_cols), jnp.bfloat16),
            jax.ShapeDtypeStruct((rows, kv_cols), jnp.bfloat16),
        ),
        in_specs=[vmem, vmem, vmem, vmem, anywhere, anywhere],
        out_specs=(vmem, vmem, vmem),
        scratch_shapes=[
            pltpu.VMEM((q_tiles, parts * width, 256), jnp.bfloat16),
            pltpu.VMEM((2, parts * width, kv_cols), jnp.bfloat16),
            pltpu.VMEM((rows, parts * width), jnp.bfloat16),
            pltpu.VMEM((rows, HD), jnp.float32),
            pltpu.VMEM((branches * heads * steps, HD), jnp.float32),
            pltpu.SemaphoreType.DMA((q_tiles + 2,)),
        ],
        compiler_params=pltpu.CompilerParams(vmem_limit_bytes=48 * 2**20),
    )(full, gain.reshape(parts, width), cosine, sine, w_query, w_keyval)

    half_count = branches // 2
    done = []
    for part in range(2):
        partial = pl.pallas_call(
            functools.partial(attend_kernel, part * half_count, half_count),
            out_shape=jax.ShapeDtypeStruct((parts, half_count * steps, width), jnp.bfloat16),
            in_specs=[smem, smem, vmem, vmem, vmem, vmem, anywhere, anywhere, vmem],
            out_specs=vmem,
            scratch_shapes=[
                pltpu.VMEM(((groups * per + own) * 2 * page, kv_cols), jnp.bfloat16),
                pltpu.VMEM((half_count * 8, slots * page), jnp.float32),
                pltpu.VMEM((half_count * heads * steps, HD), jnp.float32),
                pltpu.VMEM((half_count * steps, HD), jnp.float32),
                pltpu.VMEM((half_count * steps, heads * HD), jnp.bfloat16),
                pltpu.SemaphoreType.DMA((groups + 1,)),
            ],
            compiler_params=pltpu.CompilerParams(vmem_limit_bytes=48 * 2**20),
            cost_estimate=pl.CostEstimate(
                flops=20 * 10**9, bytes_accessed=90 * 2**20, transcendentals=half_count * heads * steps * slots * page
            ),
        )(table.reshape(-1), lengths, query, key_new, value_new, scale, every,
          pages.reshape(own * 2 * page, kv_cols), w_out)
        done.append(lax.psum_scatter(partial, "tensor", scatter_dimension=0, tiled=False))
    return jnp.concatenate(done, axis=0).reshape(branches, steps, width)


def solution(mesh):
    return jax.shard_map(
        per_device,
        mesh=mesh,
        in_specs=(
            P("branch", None, "tensor"),
            P(),
            P(None, "tensor"),
            P(None, None, "tensor"),
            P("tensor", None),
            P("branch", None, None, "tensor"),
            P("branch", None, "tensor"),
            P("branch"),
            P(),
            P("branch", None),
            P("branch"),
        ),
        out_specs=P("branch", None, "tensor"),
        check_vma=False,
    )
```
